32 devices in a mesh: grp: 16 (over z, y, x), seg: 2 (over core).
Axes of the slice: x: 2, y: 2, z: 4, core: 2. Of those that a mesh axis runs over, the one named last changes fastest.
Arguments:
- queries: bfloat16 [32768, 384], P(('grp', 'seg')), may hold values from -16 to 16
- keys: bfloat16 [32768, 384], P(('grp', 'seg')), may hold values from -16 to 16
- values: bfloat16 [32768, 384], P(('grp', 'seg')), may hold values from -6 to 6
Outputs:
- attended: bfloat16 [32768, 384], P(('grp', 'seg'))
The draws below stay inside these ranges and needn't reach their ends.
All inputs are finite; a program needn't handle non-finite values.
Results may differ from the reference program's by a relative error of at most 0.0041.
Values may be sent and summed in bfloat16 or wider, within the bound.
A program may use at most 64 MiB of HBM per device.

```python
import jax
import jax.numpy as jnp
from jax import lax

TOK_DEV = 1024
HEADS = 6
HEAD_WIDTH = 64
SLIDE_LENGTH = 32768
SLIDE_COUNT = 1
TOKEN_TOTAL = 32768
CENTER_DILATION = 2
SEGMENT_TOKENS = 2048
WIDE_DILATION = 32


def draw_queries(key, part):
    field = 1.5 * jax.random.normal(jax.random.fold_in(key, 11), (TOKEN_TOTAL, HEADS * HEAD_WIDTH), jnp.float32)
    return jnp.clip(field, -16.0, 16.0).astype(jnp.bfloat16)


def draw_keys(key, part):
    field = jax.random.normal(jax.random.fold_in(key, 13), (TOKEN_TOTAL, HEADS * HEAD_WIDTH), jnp.float32)
    return jnp.clip(field, -16.0, 16.0).astype(jnp.bfloat16)


def levels(rng, dims, shards, low, top_value):
    gain = 1.0
    for dim, parts in shards:
        draws = jax.random.uniform(jax.random.fold_in(jax.random.fold_in(rng, 6), dim), (parts,), jnp.float32, low / len(shards), top_value / len(shards))
        gain = gain * jnp.repeat(jnp.exp(draws), dims[dim] // parts).reshape((-1,) + (1,) * (len(dims) - 1 - dim))
    return gain


def gaussian(own_key, dims, scale, limit, cuts=(), held_as=jnp.bfloat16):
    factor_of = levels(own_key, dims, cuts, -0.22, 0.18) if cuts else 1.0
    result = jax.random.normal(own_key, dims, jnp.float32) * scale * factor_of
    return jnp.minimum(jnp.maximum(result, -limit), limit).astype(held_as)


def setup_inputs(seed: int = 0) -> dict:
    seeds = jax.random.split(jax.random.key(seed), 4)
    return {
        "queries": draw_queries(jax.random.fold_in(seeds[3], 71), 0),
        "keys": draw_keys(jax.random.fold_in(seeds[3], 71), 0),
        "values": gaussian(seeds[2], (TOKEN_TOTAL, HEADS * HEAD_WIDTH), 1.0, 6.0, ((0, 32),)),
    }


def attend(query_matrix, key_matrix, value_matrix):
    scores = jnp.einsum("...nd,...md->...nm", query_matrix.astype(jnp.float32), key_matrix.astype(jnp.float32)) * (HEAD_WIDTH ** -0.5)
    highest = jnp.max(scores, axis=-1, keepdims=True)
    raised = jnp.exp(scores - highest)
    totals = jnp.sum(raised, axis=-1)
    rounded_length = lax.optimization_barrier(raised.astype(jnp.bfloat16))
    mixed = jnp.einsum("...nm,...md->...nd", rounded_length.astype(jnp.float32), value_matrix.astype(jnp.float32)) / totals[..., None]
    return mixed, highest[..., 0] + jnp.log(totals)


def blend(near_out, near_lse, center_output, center_logsumexp, center_coverage, wide_output, wide_logsumexp, wide_coverage):
    mid_level = jnp.where(center_coverage, center_logsumexp, near_lse)
    far_level = jnp.where(wide_coverage, wide_logsumexp, near_lse)
    ceiling = jnp.maximum(jnp.maximum(near_lse, mid_level), far_level)
    near_weight = jnp.exp(near_lse - ceiling)
    mid_weight = jnp.where(center_coverage, jnp.exp(mid_level - ceiling), 0.0)
    far_weight = jnp.where(wide_coverage, jnp.exp(far_level - ceiling), 0.0)
    weighted = near_weight[..., None] * near_out + mid_weight[..., None] * center_output + far_weight[..., None] * wide_output
    return weighted / (near_weight + mid_weight + far_weight)[..., None]


def run_triple(triple):
    return attend(triple[0], triple[1], triple[2])


def reference(queries, keys, values):
    results = []
    center_segments = TOKEN_TOTAL // SEGMENT_TOKENS
    center_rows = SEGMENT_TOKENS // CENTER_DILATION
    wide_rows = TOKEN_TOTAL // WIDE_DILATION
    slide_wide_rows = SLIDE_LENGTH // WIDE_DILATION
    for index_of_head in range(HEADS):
        lower = index_of_head * HEAD_WIDTH
        upper = lower + HEAD_WIDTH
        query_head = queries[:, lower:upper]
        key_head = keys[:, lower:upper]
        value_head = values[:, lower:upper]

        def blocked(source_tensor):
            return source_tensor.reshape(TOKEN_TOTAL // TOK_DEV, TOK_DEV, HEAD_WIDTH)

        near_out, near_lse = lax.map(run_triple, (blocked(query_head), blocked(key_head), blocked(value_head)))
        near_out = near_out.reshape(TOKEN_TOTAL, HEAD_WIDTH)
        near_lse = near_lse.reshape(TOKEN_TOTAL)

        center_shift = index_of_head % CENTER_DILATION

        def middle(source_tensor):
            return source_tensor.reshape(center_segments, center_rows, CENTER_DILATION, HEAD_WIDTH)[:, :, center_shift]

        center_output, center_logsumexp = lax.map(run_triple, (middle(query_head), middle(key_head), middle(value_head)))
        center_flags = jnp.arange(CENTER_DILATION) == center_shift
        center_coverage = jnp.broadcast_to(center_flags, (center_segments, center_rows, CENTER_DILATION)).reshape(TOKEN_TOTAL)
        center_output_full = jnp.broadcast_to(center_output[:, :, None, :], (center_segments, center_rows, CENTER_DILATION, HEAD_WIDTH)).reshape(TOKEN_TOTAL, HEAD_WIDTH)
        center_logsumexp_full = jnp.broadcast_to(center_logsumexp[:, :, None], (center_segments, center_rows, CENTER_DILATION)).reshape(TOKEN_TOTAL)

        wide_shift = index_of_head % WIDE_DILATION

        def distant(source_tensor):
            return source_tensor.reshape(SLIDE_COUNT, slide_wide_rows, WIDE_DILATION, HEAD_WIDTH)[:, :, wide_shift]

        wide_output, wide_logsumexp = lax.map(run_triple, (distant(query_head), distant(key_head), distant(value_head)))
        wide_output = wide_output.reshape(wide_rows, HEAD_WIDTH)
        wide_logsumexp = wide_logsumexp.reshape(wide_rows)
        wide_flags = jnp.arange(WIDE_DILATION) == wide_shift
        wide_coverage = jnp.broadcast_to(wide_flags, (wide_rows, WIDE_DILATION)).reshape(TOKEN_TOTAL)
        wide_output_full = jnp.broadcast_to(wide_output[:, None, :], (wide_rows, WIDE_DILATION, HEAD_WIDTH)).reshape(TOKEN_TOTAL, HEAD_WIDTH)
        wide_logsumexp_full = jnp.broadcast_to(wide_logsumexp[:, None], (wide_rows, WIDE_DILATION)).reshape(TOKEN_TOTAL)

        results.append(blend(near_out, near_lse, center_output_full, center_logsumexp_full, center_coverage, wide_output_full, wide_logsumexp_full, wide_coverage))
    stacked = jnp.stack(results, axis=1)
    return stacked.reshape(TOKEN_TOTAL, HEADS * HEAD_WIDTH).astype(jnp.bfloat16)
```

```python
import functools

import jax
import jax.numpy as jnp
from jax import lax
from jax.experimental import pallas as pl
from jax.experimental.pallas import tpu as pltpu
from jax.sharding import PartitionSpec as P

HEAD_WIDTH = 64
PAIR = 2 * HEAD_WIDTH
SLIDE_GRP = 16
BLOCK = 256

MESH = pl.DeviceIdType.MESH
F32 = jnp.float32
BF16 = jnp.bfloat16


def scores_of(query, key):
    return lax.dot_general(query, key, (((1,), (1,)), ((), ())), preferred_element_type=F32)


def attend(query, keys, values):
    scores = [scores_of(query, key) for key in keys]
    highest = functools.reduce(
        jnp.maximum, [jnp.max(one, axis=-1, keepdims=True) for one in scores]
    )
    total = None
    for one, value in zip(scores, values):
        raised = jnp.exp(one - highest).astype(BF16)
        part = jnp.dot(raised, value, preferred_element_type=F32)
        total = part if total is None else total + part
    return total, highest


def divide(total):
    return total / pltpu.roll(total, HEAD_WIDTH, 1)


def kernel(
    seg_count,
    q_ref, k_ref, v_ref, o_ref,
    q32, k32, v32, qm, kp, va, vb, mid_out, mid_in, vmid, far, outp, acc_s, max_s,
    mid_send, mid_recv, far_send, far_recv, fwd_send, fwd_recv,
):
    rows = q_ref.shape[0]
    pairs = q_ref.shape[1] // PAIR
    mid = rows // seg_count
    period = SLIDE_GRP * seg_count
    far_rows = rows // period
    far_pad = far.shape[4]
    block = min(BLOCK, mid)
    grp, seg = lax.axis_index("grp"), lax.axis_index("seg")
    place = lax.rem(grp, SLIDE_GRP)
    base = grp - place

    barrier = pltpu.get_barrier_semaphore()
    for step in range(1, SLIDE_GRP):
        peer = base + lax.rem(place + step, SLIDE_GRP)
        pl.semaphore_signal(barrier, inc=1, device_id=(peer, seg), device_id_type=MESH)
    for step in range(1, seg_count):
        peer = lax.rem(seg + step, seg_count)
        pl.semaphore_signal(barrier, inc=1, device_id=(grp, peer), device_id_type=MESH)

    def left_of(count):
        return lax.broadcasted_iota(jnp.int32, (count, PAIR), 1) < HEAD_WIDTH

    left = left_of(mid)
    far_left = left_of(far_rows)

    def far_slot(array, pair):
        picked = jnp.where(
            far_left,
            array[pair, pl.ds((2 * pair) % period, far_rows, stride=period), :],
            array[pair, pl.ds((2 * pair + 1) % period, far_rows, stride=period), :],
        )
        if far_pad > far_rows:
            picked = jnp.concatenate([picked] * (far_pad // far_rows), axis=0)
        return picked.astype(BF16)

    for pair in range(pairs):
        columns = slice(pair * PAIR, (pair + 1) * PAIR)
        even, odd = (2 * pair) % seg_count, (2 * pair + 1) % seg_count
        k32[pair] = k_ref[:, columns].astype(F32)
        v32[pair] = v_ref[:, columns].astype(F32)
        mid_out[0, pair] = jnp.where(
            left,
            k32[pair, pl.ds(even, mid, stride=seg_count), :],
            k32[pair, pl.ds(odd, mid, stride=seg_count), :],
        ).astype(BF16)
        mid_out[1, pair] = jnp.where(
            left,
            v32[pair, pl.ds(even, mid, stride=seg_count), :],
            v32[pair, pl.ds(odd, mid, stride=seg_count), :],
        ).astype(BF16)
        far[seg, place, 0, pair] = far_slot(k32, pair)
        far[seg, place, 1, pair] = far_slot(v32, pair)

    pl.semaphore_wait(barrier, SLIDE_GRP - 1 + seg_count - 1)

    mid_copies = []
    for step in range(1, seg_count):
        peer = lax.rem(seg + step, seg_count)
        copy = pltpu.make_async_remote_copy(
            src_ref=mid_out,
            dst_ref=mid_in.at[seg_count - 1 - step],
            send_sem=mid_send.at[step - 1],
            recv_sem=mid_recv.at[seg_count - 1 - step],
            device_id=(grp, peer),
            device_id_type=MESH,
        )
        copy.start()
        mid_copies.append(copy)
    far_copies = []
    for step in range(1, SLIDE_GRP):
        peer = base + lax.rem(place + step, SLIDE_GRP)
        copy = pltpu.make_async_remote_copy(
            src_ref=far.at[seg, place],
            dst_ref=far.at[seg, place],
            send_sem=far_send.at[step - 1],
            recv_sem=far_recv.at[SLIDE_GRP - 1 - step],
            device_id=(peer, seg),
            device_id_type=MESH,
        )
        copy.start()
        far_copies.append(copy)

    for pair in range(pairs):
        columns = slice(pair * PAIR, (pair + 1) * PAIR)
        q32[pair] = q_ref[:, columns].astype(F32) * HEAD_WIDTH ** (-0.5)
        for residue in range(seg_count):
            target = pl.ds(residue * mid, mid)
            source = pl.ds(residue, mid, stride=seg_count)
            query = q32[pair, source, :]
            qm[2 * pair, target] = jnp.where(left, query, 0.0).astype(BF16)
            qm[2 * pair + 1, target] = jnp.where(left, 0.0, query).astype(BF16)
            kp[pair, target] = k32[pair, source, :].astype(BF16)
            value = v32[pair, source, :]
            for side in range(2):
                head = 2 * pair + side
                full = jnp.where(left, value, 1.0) if side == 0 else jnp.where(left, 1.0, value)
                va[head, target] = full.astype(BF16)
                if residue == head % seg_count:
                    full = full * 2.0
                vb[head, target] = full.astype(BF16)

    def lanes(side):
        return slice(side * HEAD_WIDTH, (side + 1) * HEAD_WIDTH)

    outer_blocks = (rows - mid) // block

    def outer(index, carry):
        pair = index // outer_blocks
        part = index % outer_blocks
        for side in range(2):
            head = 2 * pair + side
            own = head % seg_count
            start = ((own + 1) * mid + part * block) % rows
            target = pl.ds(pl.multiple_of(start, block), block)
            total, _ = attend(qm[head, target], [kp[pair]], [va[head]])
            outp[pair, target, lanes(side)] = divide(total)[:, lanes(side)]
        return carry

    lax.fori_loop(0, pairs * outer_blocks, outer, 0)

    for copy in mid_copies:
        copy.wait()
    away = (seg_count - 1) * mid
    away_left = left_of(away)
    for pair in range(pairs):
        value = mid_in[:, 1, pair].reshape(away, PAIR).astype(F32)
        vmid[2 * pair] = jnp.where(away_left, value, 1.0).astype(BF16)
        vmid[2 * pair + 1] = jnp.where(away_left, 1.0, value).astype(BF16)

    inner_blocks = mid // block

    def inner(index, carry):
        pair = index // inner_blocks
        part = index % inner_blocks
        away_keys = mid_in[:, 0, pair].reshape(away, PAIR)
        for side in range(2):
            head = 2 * pair + side
            own = head % seg_count
            start = own * mid + part * block
            target = pl.ds(pl.multiple_of(start, block), block)
            total, highest = attend(
                qm[head, target], [kp[pair], away_keys], [vb[head], vmid[head]]
            )
            outp[pair, target, lanes(side)] = divide(total)[:, lanes(side)]
            kept = pl.ds(pl.multiple_of(part * block, block), block)
            acc_s[head, kept] = total
            max_s[head, kept] = jnp.broadcast_to(highest, (block, PAIR))
        return carry

    early = (pairs - 1) * inner_blocks
    lax.fori_loop(0, early, inner, 0)

    for copy in far_copies:
        copy.wait()
    fwd_copies = []
    for step in range(1, seg_count):
        peer = lax.rem(seg + step, seg_count)
        copy = pltpu.make_async_remote_copy(
            src_ref=far.at[seg],
            dst_ref=far.at[seg],
            send_sem=fwd_send.at[step - 1],
            recv_sem=fwd_recv.at[seg_count - 1 - step],
            device_id=(grp, peer),
            device_id_type=MESH,
        )
        copy.start()
        fwd_copies.append(copy)
    lax.fori_loop(early, pairs * inner_blocks, inner, 0)
    for copy in fwd_copies:
        copy.wait()

    far_keys_count = seg_count * SLIDE_GRP * far_pad
    wide_left = left_of(far_keys_count)
    for pair in range(pairs):
        far_keys = far[:, :, 0, pair].reshape(far_keys_count, PAIR)
        far_values = far[:, :, 1, pair].reshape(far_keys_count, PAIR).astype(F32)
        for side in range(2):
            head = 2 * pair + side
            query = q32[pair, pl.ds(head % period, far_rows, stride=period), :]
            query = jnp.where(far_left == (side == 0), query, 0.0)
            if far_pad > far_rows:
                query = jnp.concatenate([query] * (far_pad // far_rows), axis=0)
            value = jnp.where(wide_left == (side == 0), far_values, 1.0)
            if far_pad > far_rows:
                within = lax.broadcasted_iota(jnp.int32, (far_keys_count, PAIR), 0) % far_pad
                value = jnp.where(within < far_rows, value, 0.0)
            total, highest = attend(query.astype(BF16), [far_keys], [value.astype(BF16)])
            total, highest = total[:far_rows], highest[:far_rows]
            ours = pl.ds(head // seg_count % SLIDE_GRP, far_rows, stride=SLIDE_GRP)
            near_total, near_highest = acc_s[head, ours, :], max_s[head, ours, :]
            ceiling = jnp.maximum(near_highest, highest)
            joined = near_total * jnp.exp(near_highest - ceiling) + total * jnp.exp(
                highest - ceiling
            )
            place_rows = pl.ds(
                head % seg_count * mid + head // seg_count % SLIDE_GRP, far_rows, stride=SLIDE_GRP
            )
            outp[pair, place_rows, :] = jnp.where(
                far_left == (side == 0), divide(joined), outp[pair, place_rows, :]
            )

    for pair in range(pairs):
        columns = slice(pair * PAIR, (pair + 1) * PAIR)
        for residue in range(seg_count):
            k32[pair, pl.ds(residue, mid, stride=seg_count), :] = outp[
                pair, pl.ds(residue * mid, mid)
            ]
        o_ref[:, columns] = k32[pair].astype(BF16)


def body(queries, keys, values):
    rows, features = queries.shape
    seg_count = lax.axis_size("seg")
    pairs = features // PAIR
    heads = features // HEAD_WIDTH
    mid = rows // seg_count
    far_rows = rows // (SLIDE_GRP * seg_count)
    far_pad = max(16, far_rows)
    away = (seg_count - 1) * mid
    vmem = pl.BlockSpec(memory_space=pltpu.VMEM)
    dma = pltpu.SemaphoreType.DMA
    return pl.pallas_call(
        functools.partial(kernel, seg_count),
        out_shape=jax.ShapeDtypeStruct(queries.shape, BF16),
        in_specs=[vmem] * 3,
        out_specs=vmem,
        scratch_shapes=[
            pltpu.VMEM((pairs, rows, PAIR), F32),
            pltpu.VMEM((pairs, rows, PAIR), F32),
            pltpu.VMEM((pairs, rows, PAIR), F32),
            pltpu.VMEM((heads, rows, PAIR), BF16),
            pltpu.VMEM((pairs, rows, PAIR), BF16),
            pltpu.VMEM((heads, rows, PAIR), BF16),
            pltpu.VMEM((heads, rows, PAIR), BF16),
            pltpu.VMEM((2, pairs, mid, PAIR), BF16),
            pltpu.VMEM((seg_count - 1, 2, pairs, mid, PAIR), BF16),
            pltpu.VMEM((heads, away, PAIR), BF16),
            pltpu.VMEM((seg_count, SLIDE_GRP, 2, pairs, far_pad, PAIR), BF16),
            pltpu.VMEM((pairs, rows, PAIR), F32),
            pltpu.VMEM((heads, mid, PAIR), F32),
            pltpu.VMEM((heads, mid, PAIR), F32),
            dma((seg_count - 1,)),
            dma((seg_count - 1,)),
            dma((SLIDE_GRP - 1,)),
            dma((SLIDE_GRP - 1,)),
            dma((seg_count - 1,)),
            dma((seg_count - 1,)),
        ],
        compiler_params=pltpu.CompilerParams(
            collective_id=0, has_side_effects=True, vmem_limit_bytes=56 * 1024 * 1024
        ),
        name="dilated_attention",
    )(queries, keys, values)


def solution(mesh):
    spec = P(("grp", "seg"), None)
    return jax.shard_map(
        body, mesh=mesh, in_specs=(spec, spec, spec), out_specs=spec, check_vma=False
    )
```

```python
import functools

import jax
import jax.numpy as jnp
from jax import lax
from jax.experimental import pallas as pl
from jax.experimental.pallas import tpu as pltpu
from jax.sharding import PartitionSpec as P

HEAD_WIDTH = 64
PAIR = 2 * HEAD_WIDTH
SLIDE_GRP = 16
LINE = 4
PLANE = SLIDE_GRP // LINE
BLOCK = 256

MESH = pl.DeviceIdType.MESH
F32 = jnp.float32
BF16 = jnp.bfloat16


def scores_of(query, key):
    return lax.dot_general(query, key, (((1,), (1,)), ((), ())), preferred_element_type=F32)


def attend(jobs):
    def scores(job):
        query, keys, _ = job
        return [scores_of(query, key) for key in keys]

    results = []
    ahead = scores(jobs[0])
    for index, (_, _, values) in enumerate(jobs):
        now = ahead
        if index + 1 < len(jobs):
            ahead = scores(jobs[index + 1])
        highest = functools.reduce(
            jnp.maximum, [jnp.max(one, axis=-1, keepdims=True) for one in now]
        )
        total = None
        for one, value in zip(now, values):
            raised = jnp.exp(one - highest).astype(BF16)
            part = jnp.dot(raised, value, preferred_element_type=F32)
            total = part if total is None else total + part
        results.append((total, highest))
    return results


def divide(total):
    return total / pltpu.roll(total, HEAD_WIDTH, 1)


def kernel(
    seg_count,
    q_ref, k_ref, v_ref, o_ref,
    q32, k32, v32, qm, kp, va, vb, mid_out, mid_in, vmid, far, outp, acc_s, max_s,
    mid_send, mid_recv, line_send, line_recv, plane_send, plane_recv, fwd_send, fwd_recv,
):
    rows = q_ref.shape[0]
    pairs = q_ref.shape[1] // PAIR
    mid = rows // seg_count
    period = SLIDE_GRP * seg_count
    far_rows = rows // period
    far_pad = far.shape[5]
    block = min(BLOCK, mid)
    grp, seg = lax.axis_index("grp"), lax.axis_index("seg")
    place = lax.rem(grp, SLIDE_GRP)
    base = grp - place
    line, plane = place // PLANE, lax.rem(place, PLANE)

    barrier = pltpu.get_barrier_semaphore()
    line_peers = [
        base + lax.rem(line + step, LINE) * PLANE + plane for step in range(1, LINE)
    ]
    plane_peers = [
        base + line * PLANE + lax.rem(plane + step, PLANE) for step in range(1, PLANE)
    ]
    for peer in line_peers + plane_peers:
        pl.semaphore_signal(barrier, inc=1, device_id=(peer, seg), device_id_type=MESH)
    for step in range(1, seg_count):
        peer = lax.rem(seg + step, seg_count)
        pl.semaphore_signal(barrier, inc=1, device_id=(grp, peer), device_id_type=MESH)

    def left_of(count):
        return lax.broadcasted_iota(jnp.int32, (count, PAIR), 1) < HEAD_WIDTH

    left = left_of(mid)
    far_left = left_of(far_rows)

    def far_slot(array, pair):
        picked = jnp.where(
            far_left,
            array[pair, pl.ds((2 * pair) % period, far_rows, stride=period), :],
            array[pair, pl.ds((2 * pair + 1) % period, far_rows, stride=period), :],
        )
        if far_pad > far_rows:
            picked = jnp.concatenate([picked] * (far_pad // far_rows), axis=0)
        return picked.astype(BF16)

    for pair in range(pairs):
        columns = slice(pair * PAIR, (pair + 1) * PAIR)
        even, odd = (2 * pair) % seg_count, (2 * pair + 1) % seg_count
        k32[pair] = k_ref[:, columns].astype(F32)
        v32[pair] = v_ref[:, columns].astype(F32)
        mid_out[0, pair] = jnp.where(
            left,
            k32[pair, pl.ds(even, mid, stride=seg_count), :],
            k32[pair, pl.ds(odd, mid, stride=seg_count), :],
        ).astype(BF16)
        mid_out[1, pair] = jnp.where(
            left,
            v32[pair, pl.ds(even, mid, stride=seg_count), :],
            v32[pair, pl.ds(odd, mid, stride=seg_count), :],
        ).astype(BF16)
        far[seg, plane, line, 0, pair] = far_slot(k32, pair)
        far[seg, plane, line, 1, pair] = far_slot(v32, pair)

    pl.semaphore_wait(barrier, LINE - 1 + PLANE - 1 + seg_count - 1)

    mid_copies = []
    for step in range(1, seg_count):
        peer = lax.rem(seg + step, seg_count)
        copy = pltpu.make_async_remote_copy(
            src_ref=mid_out,
            dst_ref=mid_in.at[seg_count - 1 - step],
            send_sem=mid_send.at[step - 1],
            recv_sem=mid_recv.at[seg_count - 1 - step],
            device_id=(grp, peer),
            device_id_type=MESH,
        )
        copy.start()
        mid_copies.append(copy)
    line_copies = []
    for step, peer in enumerate(line_peers):
        copy = pltpu.make_async_remote_copy(
            src_ref=far.at[seg, plane, line],
            dst_ref=far.at[seg, plane, line],
            send_sem=line_send.at[step],
            recv_sem=line_recv.at[LINE - 2 - step],
            device_id=(peer, seg),
            device_id_type=MESH,
        )
        copy.start()
        line_copies.append(copy)

    for pair in range(pairs):
        columns = slice(pair * PAIR, (pair + 1) * PAIR)
        q32[pair] = q_ref[:, columns].astype(F32) * HEAD_WIDTH ** (-0.5)
        for residue in range(seg_count):
            target = pl.ds(residue * mid, mid)
            source = pl.ds(residue, mid, stride=seg_count)
            query = q32[pair, source, :]
            qm[2 * pair, target] = jnp.where(left, query, 0.0).astype(BF16)
            qm[2 * pair + 1, target] = jnp.where(left, 0.0, query).astype(BF16)
            kp[pair, target] = k32[pair, source, :].astype(BF16)
            value = v32[pair, source, :]
            for side in range(2):
                head = 2 * pair + side
                full = jnp.where(left, value, 1.0) if side == 0 else jnp.where(left, 1.0, value)
                va[head, target] = full.astype(BF16)
                if residue == head % seg_count:
                    full = full * 2.0
                vb[head, target] = full.astype(BF16)

    def lanes(side):
        return slice(side * HEAD_WIDTH, (side + 1) * HEAD_WIDTH)

    outer_blocks = (rows - mid) // block
    together = 2 if outer_blocks % 2 == 0 else 1

    def outer(index, carry):
        pair = index // (outer_blocks // together)
        first = index % (outer_blocks // together) * together
        jobs, targets = [], []
        for ahead in range(together):
            for side in range(2):
                head = 2 * pair + side
                own = head % seg_count
                start = ((own + 1) * mid + (first + ahead) * block) % rows
                target = pl.ds(pl.multiple_of(start, block), block)
                jobs.append((qm[head, target], [kp[pair]], [va[head]]))
                targets.append((target, side))
        for (target, side), (total, _) in zip(targets, attend(jobs)):
            outp[pair, target, lanes(side)] = divide(total)[:, lanes(side)]
        return carry

    outer_steps = outer_blocks // together
    lax.fori_loop(0, outer_steps, outer, 0)

    for copy in line_copies:
        copy.wait()
    plane_copies = []
    for step, peer in enumerate(plane_peers):
        copy = pltpu.make_async_remote_copy(
            src_ref=far.at[seg, plane],
            dst_ref=far.at[seg, plane],
            send_sem=plane_send.at[step],
            recv_sem=plane_recv.at[PLANE - 2 - step],
            device_id=(peer, seg),
            device_id_type=MESH,
        )
        copy.start()
        plane_copies.append(copy)
    lax.fori_loop(outer_steps, pairs * outer_steps, outer, 0)

    for copy in mid_copies:
        copy.wait()
    away = (seg_count - 1) * mid
    away_left = left_of(away)
    for pair in range(pairs):
        value = mid_in[:, 1, pair].reshape(away, PAIR).astype(F32)
        vmid[2 * pair] = jnp.where(away_left, value, 1.0).astype(BF16)
        vmid[2 * pair + 1] = jnp.where(away_left, 1.0, value).astype(BF16)

    inner_blocks = mid // block

    def inner(index, carry):
        pair = index // inner_blocks
        part = index % inner_blocks
        away_keys = mid_in[:, 0, pair].reshape(away, PAIR)
        kept = pl.ds(pl.multiple_of(part * block, block), block)
        jobs, targets = [], []
        for side in range(2):
            head = 2 * pair + side
            start = head % seg_count * mid + part * block
            target = pl.ds(pl.multiple_of(start, block), block)
            jobs.append((qm[head, target], [kp[pair], away_keys], [vb[head], vmid[head]]))
            targets.append((head, target, side))
        for (head, target, side), (total, highest) in zip(targets, attend(jobs)):
            outp[pair, target, lanes(side)] = divide(total)[:, lanes(side)]
            acc_s[head, kept] = total
            max_s[head, kept] = jnp.broadcast_to(highest, (block, PAIR))
        return carry

    early = (pairs - 1) * inner_blocks
    lax.fori_loop(0, early, inner, 0)

    for copy in plane_copies:
        copy.wait()
    fwd_copies = []
    for step in range(1, seg_count):
        peer = lax.rem(seg + step, seg_count)
        copy = pltpu.make_async_remote_copy(
            src_ref=far.at[seg],
            dst_ref=far.at[seg],
            send_sem=fwd_send.at[step - 1],
            recv_sem=fwd_recv.at[seg_count - 1 - step],
            device_id=(grp, peer),
            device_id_type=MESH,
        )
        copy.start()
        fwd_copies.append(copy)
    lax.fori_loop(early, pairs * inner_blocks, inner, 0)
    for copy in fwd_copies:
        copy.wait()

    far_keys_count = seg_count * SLIDE_GRP * far_pad
    wide_left = left_of(far_keys_count)
    for pair in range(pairs):
        far_keys = far[:, :, :, 0, pair].reshape(far_keys_count, PAIR)
        far_values = far[:, :, :, 1, pair].reshape(far_keys_count, PAIR).astype(F32)
        for side in range(2):
            head = 2 * pair + side
            query = q32[pair, pl.ds(head % period, far_rows, stride=period), :]
            query = jnp.where(far_left == (side == 0), query, 0.0)
            if far_pad > far_rows:
                query = jnp.concatenate([query] * (far_pad // far_rows), axis=0)
            value = jnp.where(wide_left == (side == 0), far_values, 1.0)
            if far_pad > far_rows:
                within = lax.broadcasted_iota(jnp.int32, (far_keys_count, PAIR), 0) % far_pad
                value = jnp.where(within < far_rows, value, 0.0)
            (total, highest), = attend([(query.astype(BF16), [far_keys], [value.astype(BF16)])])
            total, highest = total[:far_rows], highest[:far_rows]
            ours = pl.ds(head // seg_count % SLIDE_GRP, far_rows, stride=SLIDE_GRP)
            near_total, near_highest = acc_s[head, ours, :], max_s[head, ours, :]
            ceiling = jnp.maximum(near_highest, highest)
            joined = near_total * jnp.exp(near_highest - ceiling) + total * jnp.exp(
                highest - ceiling
            )
            place_rows = pl.ds(
                head % seg_count * mid + head // seg_count % SLIDE_GRP, far_rows, stride=SLIDE_GRP
            )
            outp[pair, place_rows, :] = jnp.where(
                far_left == (side == 0), divide(joined), outp[pair, place_rows, :]
            )

    o_ref[...] = outp[...].astype(BF16)


def unsort(seg_count, sorted_ref, o_ref, stage):
    pairs, rows, _ = sorted_ref.shape
    mid = rows // seg_count
    for pair in range(pairs):
        for residue in range(seg_count):
            stage[pair, pl.ds(residue, mid, stride=seg_count), :] = sorted_ref[
                pair, pl.ds(residue * mid, mid)
            ].astype(F32)
        o_ref[:, pair * PAIR : (pair + 1) * PAIR] = stage[pair].astype(BF16)


def body(queries, keys, values):
    rows, features = queries.shape
    seg_count = lax.axis_size("seg")
    pairs = features // PAIR
    heads = features // HEAD_WIDTH
    mid = rows // seg_count
    far_rows = rows // (SLIDE_GRP * seg_count)
    far_pad = max(16, far_rows)
    away = (seg_count - 1) * mid
    vmem = pl.BlockSpec(memory_space=pltpu.VMEM)
    dma = pltpu.SemaphoreType.DMA
    ordered = pl.pallas_call(
        functools.partial(kernel, seg_count),
        out_shape=jax.ShapeDtypeStruct((pairs, rows, PAIR), BF16),
        in_specs=[vmem] * 3,
        out_specs=vmem,
        scratch_shapes=[
            pltpu.VMEM((pairs, rows, PAIR), F32),
            pltpu.VMEM((pairs, rows, PAIR), F32),
            pltpu.VMEM((pairs, rows, PAIR), F32),
            pltpu.VMEM((heads, rows, PAIR), BF16),
            pltpu.VMEM((pairs, rows, PAIR), BF16),
            pltpu.VMEM((heads, rows, PAIR), BF16),
            pltpu.VMEM((heads, rows, PAIR), BF16),
            pltpu.VMEM((2, pairs, mid, PAIR), BF16),
            pltpu.VMEM((seg_count - 1, 2, pairs, mid, PAIR), BF16),
            pltpu.VMEM((heads, away, PAIR), BF16),
            pltpu.VMEM((seg_count, PLANE, LINE, 2, pairs, far_pad, PAIR), BF16),
            pltpu.VMEM((pairs, rows, PAIR), F32),
            pltpu.VMEM((heads, mid, PAIR), F32),
            pltpu.VMEM((heads, mid, PAIR), F32),
            dma((seg_count - 1,)),
            dma((seg_count - 1,)),
            dma((LINE - 1,)),
            dma((LINE - 1,)),
            dma((PLANE - 1,)),
            dma((PLANE - 1,)),
            dma((seg_count - 1,)),
            dma((seg_count - 1,)),
        ],
        compiler_params=pltpu.CompilerParams(
            collective_id=0, has_side_effects=True, vmem_limit_bytes=56 * 1024 * 1024
        ),
        name="dilated_attention",
    )(queries, keys, values)
    return pl.pallas_call(
        functools.partial(unsort, seg_count),
        out_shape=jax.ShapeDtypeStruct(queries.shape, BF16),
        in_specs=[vmem],
        out_specs=vmem,
        scratch_shapes=[pltpu.VMEM((pairs, rows, PAIR), F32)],
        compiler_params=pltpu.CompilerParams(vmem_limit_bytes=32 * 1024 * 1024),
        name="token_order",
    )(ordered)


def solution(mesh):
    spec = P(("grp", "seg"), None)
    return jax.shard_map(
        body, mesh=mesh, in_specs=(spec, spec, spec), out_specs=spec, check_vma=False
    )
```

```python
import functools

import jax
import jax.numpy as jnp
from jax import lax
from jax.experimental import pallas as pl
from jax.experimental.pallas import tpu as pltpu
from jax.sharding import PartitionSpec as P

HEAD_WIDTH = 64
PAIR = 2 * HEAD_WIDTH
SLIDE_GRP = 16
LINE = 4
PLANE = SLIDE_GRP // LINE
BLOCK = 256

MESH = pl.DeviceIdType.MESH
F32 = jnp.float32
BF16 = jnp.bfloat16


def scores_of(query, key):
    return lax.dot_general(query, key, (((1,), (1,)), ((), ())), preferred_element_type=F32)


def attend(jobs):
    def scores(job):
        query, keys, _ = job
        return [scores_of(query, key) for key in keys]

    results = []
    ahead = scores(jobs[0])
    for index, (_, _, values) in enumerate(jobs):
        now = ahead
        if index + 1 < len(jobs):
            ahead = scores(jobs[index + 1])
        highest = functools.reduce(
            jnp.maximum, [jnp.max(one, axis=-1, keepdims=True) for one in now]
        )
        total = None
        for one, value in zip(now, values):
            raised = jnp.exp(one - highest).astype(BF16)
            part = jnp.dot(raised, value, preferred_element_type=F32)
            total = part if total is None else total + part
        results.append((total, highest))
    return results


def divide(total):
    return total / pltpu.roll(total, HEAD_WIDTH, 1)


def kernel(
    seg_count,
    q_ref, k_ref, v_ref, o_ref,
    q32, k32, v32, qm, kp, va, vb, mid_out, mid_in, vmid, far, outp, acc_s, max_s,
    mid_send, mid_recv, line_send, line_recv, plane_send, plane_recv, fwd_send, fwd_recv,
):
    rows = q_ref.shape[0]
    pairs = q_ref.shape[1] // PAIR
    mid = rows // seg_count
    period = SLIDE_GRP * seg_count
    far_rows = rows // period
    far_pad = far.shape[5]
    block = min(BLOCK, mid)
    grp, seg = lax.axis_index("grp"), lax.axis_index("seg")
    place = lax.rem(grp, SLIDE_GRP)
    base = grp - place
    line, plane = place // PLANE, lax.rem(place, PLANE)

    barrier = pltpu.get_barrier_semaphore()
    line_peers = [
        base + lax.rem(line + step, LINE) * PLANE + plane for step in range(1, LINE)
    ]
    plane_peers = [
        base + line * PLANE + lax.rem(plane + step, PLANE) for step in range(1, PLANE)
    ]
    for peer in line_peers + plane_peers:
        pl.semaphore_signal(barrier, inc=1, device_id=(peer, seg), device_id_type=MESH)
    for step in range(1, seg_count):
        peer = lax.rem(seg + step, seg_count)
        pl.semaphore_signal(barrier, inc=1, device_id=(grp, peer), device_id_type=MESH)

    def left_of(count):
        return lax.broadcasted_iota(jnp.int32, (count, PAIR), 1) < HEAD_WIDTH

    left = left_of(mid)
    far_left = left_of(far_rows)

    def far_slot(array, pair):
        picked = jnp.where(
            far_left,
            array[pair, pl.ds((2 * pair) % period, far_rows, stride=period), :],
            array[pair, pl.ds((2 * pair + 1) % period, far_rows, stride=period), :],
        )
        if far_pad > far_rows:
            picked = jnp.concatenate([picked] * (far_pad // far_rows), axis=0)
        return picked.astype(BF16)

    for pair in range(pairs):
        columns = slice(pair * PAIR, (pair + 1) * PAIR)
        even, odd = (2 * pair) % seg_count, (2 * pair + 1) % seg_count
        k32[pair] = k_ref[:, columns].astype(F32)
        v32[pair] = v_ref[:, columns].astype(F32)
        mid_out[0, pair] = jnp.where(
            left,
            k32[pair, pl.ds(even, mid, stride=seg_count), :],
            k32[pair, pl.ds(odd, mid, stride=seg_count), :],
        ).astype(BF16)
        mid_out[1, pair] = jnp.where(
            left,
            v32[pair, pl.ds(even, mid, stride=seg_count), :],
            v32[pair, pl.ds(odd, mid, stride=seg_count), :],
        ).astype(BF16)
        far[seg, plane, line, 0, pair] = far_slot(k32, pair)
        far[seg, plane, line, 1, pair] = far_slot(v32, pair)

    pl.semaphore_wait(barrier, LINE - 1 + PLANE - 1 + seg_count - 1)

    mid_copies = []
    for step in range(1, seg_count):
        peer = lax.rem(seg + step, seg_count)
        copy = pltpu.make_async_remote_copy(
            src_ref=mid_out,
            dst_ref=mid_in.at[seg_count - 1 - step],
            send_sem=mid_send.at[step - 1],
            recv_sem=mid_recv.at[seg_count - 1 - step],
            device_id=(grp, peer),
            device_id_type=MESH,
        )
        copy.start()
        mid_copies.append(copy)
    line_copies = []
    for step, peer in enumerate(line_peers):
        copy = pltpu.make_async_remote_copy(
            src_ref=far.at[seg, plane, line],
            dst_ref=far.at[seg, plane, line],
            send_sem=line_send.at[step],
            recv_sem=line_recv.at[LINE - 2 - step],
            device_id=(peer, seg),
            device_id_type=MESH,
        )
        copy.start()
        line_copies.append(copy)

    for pair in range(pairs):
        columns = slice(pair * PAIR, (pair + 1) * PAIR)
        q32[pair] = q_ref[:, columns].astype(F32) * HEAD_WIDTH ** (-0.5)
        for residue in range(seg_count):
            target = pl.ds(residue * mid, mid)
            source = pl.ds(residue, mid, stride=seg_count)
            query = q32[pair, source, :]
            qm[2 * pair, target] = jnp.where(left, query, 0.0).astype(BF16)
            qm[2 * pair + 1, target] = jnp.where(left, 0.0, query).astype(BF16)
            kp[pair, target] = k32[pair, source, :].astype(BF16)
            value = v32[pair, source, :]
            for side in range(2):
                head = 2 * pair + side
                full = jnp.where(left, value, 1.0) if side == 0 else jnp.where(left, 1.0, value)
                va[head, target] = full.astype(BF16)
                if residue == head % seg_count:
                    full = full * 2.0
                vb[head, target] = full.astype(BF16)

    def lanes(side):
        return slice(side * HEAD_WIDTH, (side + 1) * HEAD_WIDTH)

    outer_blocks = (rows - mid) // block
    together = 2 if outer_blocks % 2 == 0 else 1

    def outer(index, carry):
        pair = index // (outer_blocks // together)
        first = index % (outer_blocks // together) * together
        jobs, targets = [], []
        for ahead in range(together):
            for side in range(2):
                head = 2 * pair + side
                own = head % seg_count
                start = ((own + 1) * mid + (first + ahead) * block) % rows
                target = pl.ds(pl.multiple_of(start, block), block)
                jobs.append((qm[head, target], [kp[pair]], [va[head]]))
                targets.append((target, side))
        for (target, side), (total, _) in zip(targets, attend(jobs)):
            outp[pair, target, lanes(side)] = divide(total)[:, lanes(side)]
        return carry

    outer_steps = outer_blocks // together
    lax.fori_loop(0, outer_steps, outer, 0)

    for copy in line_copies:
        copy.wait()
    plane_copies = []
    for step, peer in enumerate(plane_peers):
        copy = pltpu.make_async_remote_copy(
            src_ref=far.at[seg, plane],
            dst_ref=far.at[seg, plane],
            send_sem=plane_send.at[step],
            recv_sem=plane_recv.at[PLANE - 2 - step],
            device_id=(peer, seg),
            device_id_type=MESH,
        )
        copy.start()
        plane_copies.append(copy)
    lax.fori_loop(outer_steps, pairs * outer_steps, outer, 0)

    for copy in mid_copies:
        copy.wait()
    away = (seg_count - 1) * mid
    away_left = left_of(away)
    for pair in range(pairs):
        value = mid_in[:, 1, pair].reshape(away, PAIR).astype(F32)
        vmid[2 * pair] = jnp.where(away_left, value, 1.0).astype(BF16)
        vmid[2 * pair + 1] = jnp.where(away_left, 1.0, value).astype(BF16)

    inner_blocks = mid // block

    def inner(pair, carry):
        away_keys = mid_in[:, 0, pair].reshape(away, PAIR)
        jobs, targets = [], []
        for part in range(inner_blocks):
            for side in range(2):
                head = 2 * pair + side
                start = head % seg_count * mid + part * block
                target = pl.ds(pl.multiple_of(start, block), block)
                jobs.append((qm[head, target], [kp[pair], away_keys], [vb[head], vmid[head]]))
                targets.append((head, target, side, pl.ds(part * block, block)))
        for (head, target, side, kept), (total, highest) in zip(targets, attend(jobs)):
            outp[pair, target, lanes(side)] = divide(total)[:, lanes(side)]
            acc_s[head, kept] = total
            max_s[head, kept] = jnp.broadcast_to(highest, (block, PAIR))
        return carry

    early = pairs - 1
    lax.fori_loop(0, early, inner, 0)

    for copy in plane_copies:
        copy.wait()
    fwd_copies = []
    for step in range(1, seg_count):
        peer = lax.rem(seg + step, seg_count)
        copy = pltpu.make_async_remote_copy(
            src_ref=far.at[seg],
            dst_ref=far.at[seg],
            send_sem=fwd_send.at[step - 1],
            recv_sem=fwd_recv.at[seg_count - 1 - step],
            device_id=(grp, peer),
            device_id_type=MESH,
        )
        copy.start()
        fwd_copies.append(copy)
    lax.fori_loop(early, pairs, inner, 0)
    for copy in fwd_copies:
        copy.wait()

    far_keys_count = seg_count * SLIDE_GRP * far_pad
    wide_left = left_of(far_keys_count)
    jobs = []
    for pair in range(pairs):
        far_keys = far[:, :, :, 0, pair].reshape(far_keys_count, PAIR)
        far_values = far[:, :, :, 1, pair].reshape(far_keys_count, PAIR).astype(F32)
        for side in range(2):
            head = 2 * pair + side
            query = q32[pair, pl.ds(head % period, far_rows, stride=period), :]
            query = jnp.where(far_left == (side == 0), query, 0.0)
            if far_pad > far_rows:
                query = jnp.concatenate([query] * (far_pad // far_rows), axis=0)
            value = jnp.where(wide_left == (side == 0), far_values, 1.0)
            if far_pad > far_rows:
                within = lax.broadcasted_iota(jnp.int32, (far_keys_count, PAIR), 0) % far_pad
                value = jnp.where(within < far_rows, value, 0.0)
            jobs.append((query.astype(BF16), [far_keys], [value.astype(BF16)]))

    results = attend(jobs)
    for pair in range(pairs):
        for side in range(2):
            head = 2 * pair + side
            total, highest = results[head]
            total, highest = total[:far_rows], highest[:far_rows]
            ours = pl.ds(head // seg_count % SLIDE_GRP, far_rows, stride=SLIDE_GRP)
            near_total, near_highest = acc_s[head, ours, :], max_s[head, ours, :]
            ceiling = jnp.maximum(near_highest, highest)
            joined = near_total * jnp.exp(near_highest - ceiling) + total * jnp.exp(
                highest - ceiling
            )
            place_rows = pl.ds(
                head % seg_count * mid + head // seg_count % SLIDE_GRP, far_rows, stride=SLIDE_GRP
            )
            outp[pair, place_rows, :] = jnp.where(
                far_left == (side == 0), divide(joined), outp[pair, place_rows, :]
            )

    o_ref[...] = outp[...].astype(BF16)


def unsort(seg_count, sorted_ref, o_ref, stage):
    pairs, rows, _ = sorted_ref.shape
    mid = rows // seg_count
    for pair in range(pairs):
        for residue in range(seg_count):
            stage[pair, pl.ds(residue, mid, stride=seg_count), :] = sorted_ref[
                pair, pl.ds(residue * mid, mid)
            ].astype(F32)
        o_ref[:, pair * PAIR : (pair + 1) * PAIR] = stage[pair].astype(BF16)


def body(queries, keys, values):
    rows, features = queries.shape
    seg_count = lax.axis_size("seg")
    pairs = features // PAIR
    heads = features // HEAD_WIDTH
    mid = rows // seg_count
    far_rows = rows // (SLIDE_GRP * seg_count)
    far_pad = max(16, far_rows)
    away = (seg_count - 1) * mid
    vmem = pl.BlockSpec(memory_space=pltpu.VMEM)
    dma = pltpu.SemaphoreType.DMA
    ordered = pl.pallas_call(
        functools.partial(kernel, seg_count),
        out_shape=jax.ShapeDtypeStruct((pairs, rows, PAIR), BF16),
        in_specs=[vmem] * 3,
        out_specs=vmem,
        scratch_shapes=[
            pltpu.VMEM((pairs, rows, PAIR), F32),
            pltpu.VMEM((pairs, rows, PAIR), F32),
            pltpu.VMEM((pairs, rows, PAIR), F32),
            pltpu.VMEM((heads, rows, PAIR), BF16),
            pltpu.VMEM((pairs, rows, PAIR), BF16),
            pltpu.VMEM((heads, rows, PAIR), BF16),
            pltpu.VMEM((heads, rows, PAIR), BF16),
            pltpu.VMEM((2, pairs, mid, PAIR), BF16),
            pltpu.VMEM((seg_count - 1, 2, pairs, mid, PAIR), BF16),
            pltpu.VMEM((heads, away, PAIR), BF16),
            pltpu.VMEM((seg_count, PLANE, LINE, 2, pairs, far_pad, PAIR), BF16),
            pltpu.VMEM((pairs, rows, PAIR), F32),
            pltpu.VMEM((heads, mid, PAIR), F32),
            pltpu.VMEM((heads, mid, PAIR), F32),
            dma((seg_count - 1,)),
            dma((seg_count - 1,)),
            dma((LINE - 1,)),
            dma((LINE - 1,)),
            dma((PLANE - 1,)),
            dma((PLANE - 1,)),
            dma((seg_count - 1,)),
            dma((seg_count - 1,)),
        ],
        compiler_params=pltpu.CompilerParams(
            collective_id=0, has_side_effects=True, vmem_limit_bytes=56 * 1024 * 1024
        ),
        name="dilated_attention",
    )(queries, keys, values)
    return pl.pallas_call(
        functools.partial(unsort, seg_count),
        out_shape=jax.ShapeDtypeStruct(queries.shape, BF16),
        in_specs=[vmem],
        out_specs=vmem,
        scratch_shapes=[pltpu.VMEM((pairs, rows, PAIR), F32)],
        compiler_params=pltpu.CompilerParams(vmem_limit_bytes=32 * 1024 * 1024),
        name="token_order",
    )(ordered)


def solution(mesh):
    spec = P(("grp", "seg"), None)
    return jax.shard_map(
        body, mesh=mesh, in_specs=(spec, spec, spec), out_specs=spec, check_vma=False
    )
```

```python
import functools

import jax
import jax.numpy as jnp
from jax import lax
from jax.experimental import pallas as pl
from jax.experimental.pallas import tpu as pltpu
from jax.sharding import PartitionSpec as P

HEAD_WIDTH = 64
PAIR = 2 * HEAD_WIDTH
SLIDE_GRP = 16
LINE = 4
PLANE = SLIDE_GRP // LINE
BLOCK = 512

MESH = pl.DeviceIdType.MESH
F32 = jnp.float32
BF16 = jnp.bfloat16


def scores_of(query, key):
    return lax.dot_general(query, key, (((1,), (1,)), ((), ())), preferred_element_type=F32)


def attend(jobs):
    def scores(job):
        query, keys, _ = job
        return [scores_of(query, key) for key in keys]

    results = []
    ahead = scores(jobs[0])
    for index, (_, _, values) in enumerate(jobs):
        now = ahead
        if index + 1 < len(jobs):
            ahead = scores(jobs[index + 1])
        highest = functools.reduce(
            jnp.maximum, [jnp.max(one, axis=-1, keepdims=True) for one in now]
        )
        total = None
        for one, value in zip(now, values):
            raised = jnp.exp(one - highest).astype(BF16)
            part = jnp.dot(raised, value, preferred_element_type=F32)
            total = part if total is None else total + part
        results.append((total, highest))
    return results


def divide(total):
    return total / pltpu.roll(total, HEAD_WIDTH, 1)


def kernel(
    seg_count,
    q_ref, k_ref, v_ref, o_ref,
    q32, k32, v32, qm, kp, va, vb, mid_out, mid_in, vmid, far, outp, acc_s, max_s,
    mid_send, mid_recv, line_send, line_recv, plane_send, plane_recv, fwd_send, fwd_recv,
):
    rows = q_ref.shape[0]
    pairs = q_ref.shape[1] // PAIR
    mid = rows // seg_count
    period = SLIDE_GRP * seg_count
    far_rows = rows // period
    far_pad = far.shape[5]
    block = min(BLOCK, mid)
    grp, seg = lax.axis_index("grp"), lax.axis_index("seg")
    place = lax.rem(grp, SLIDE_GRP)
    base = grp - place
    line, plane = place // PLANE, lax.rem(place, PLANE)

    barrier = pltpu.get_barrier_semaphore()
    line_peers = [
        base + lax.rem(line + step, LINE) * PLANE + plane for step in range(1, LINE)
    ]
    plane_peers = [
        base + line * PLANE + lax.rem(plane + step, PLANE) for step in range(1, PLANE)
    ]
    for peer in line_peers + plane_peers:
        pl.semaphore_signal(barrier, inc=1, device_id=(peer, seg), device_id_type=MESH)
    for step in range(1, seg_count):
        peer = lax.rem(seg + step, seg_count)
        pl.semaphore_signal(barrier, inc=1, device_id=(grp, peer), device_id_type=MESH)

    def left_of(count):
        return lax.broadcasted_iota(jnp.int32, (count, PAIR), 1) < HEAD_WIDTH

    left = left_of(mid)
    far_left = left_of(far_rows)

    def far_slot(array, pair):
        picked = jnp.where(
            far_left,
            array[pair, pl.ds((2 * pair) % period, far_rows, stride=period), :],
            array[pair, pl.ds((2 * pair + 1) % period, far_rows, stride=period), :],
        )
        if far_pad > far_rows:
            picked = jnp.concatenate([picked] * (far_pad // far_rows), axis=0)
        return picked.astype(BF16)

    for pair in range(pairs):
        columns = slice(pair * PAIR, (pair + 1) * PAIR)
        even, odd = (2 * pair) % seg_count, (2 * pair + 1) % seg_count
        k32[pair] = k_ref[:, columns].astype(F32)
        v32[pair] = v_ref[:, columns].astype(F32)
        mid_out[0, pair] = jnp.where(
            left,
            k32[pair, pl.ds(even, mid, stride=seg_count), :],
            k32[pair, pl.ds(odd, mid, stride=seg_count), :],
        ).astype(BF16)
        mid_out[1, pair] = jnp.where(
            left,
            v32[pair, pl.ds(even, mid, stride=seg_count), :],
            v32[pair, pl.ds(odd, mid, stride=seg_count), :],
        ).astype(BF16)
        far[seg, plane, line, 0, pair] = far_slot(k32, pair)
        far[seg, plane, line, 1, pair] = far_slot(v32, pair)

    pl.semaphore_wait(barrier, LINE - 1 + PLANE - 1 + seg_count - 1)

    mid_copies = []
    for step in range(1, seg_count):
        peer = lax.rem(seg + step, seg_count)
        copy = pltpu.make_async_remote_copy(
            src_ref=mid_out,
            dst_ref=mid_in.at[seg_count - 1 - step],
            send_sem=mid_send.at[step - 1],
            recv_sem=mid_recv.at[seg_count - 1 - step],
            device_id=(grp, peer),
            device_id_type=MESH,
        )
        copy.start()
        mid_copies.append(copy)
    line_copies = []
    for step, peer in enumerate(line_peers):
        copy = pltpu.make_async_remote_copy(
            src_ref=far.at[seg, plane, line],
            dst_ref=far.at[seg, plane, line],
            send_sem=line_send.at[step],
            recv_sem=line_recv.at[LINE - 2 - step],
            device_id=(peer, seg),
            device_id_type=MESH,
        )
        copy.start()
        line_copies.append(copy)

    for pair in range(pairs):
        columns = slice(pair * PAIR, (pair + 1) * PAIR)
        q32[pair] = q_ref[:, columns].astype(F32) * HEAD_WIDTH ** (-0.5)
        for residue in range(seg_count):
            target = pl.ds(residue * mid, mid)
            source = pl.ds(residue, mid, stride=seg_count)
            query = q32[pair, source, :]
            qm[2 * pair, target] = jnp.where(left, query, 0.0).astype(BF16)
            qm[2 * pair + 1, target] = jnp.where(left, 0.0, query).astype(BF16)
            kp[pair, target] = k32[pair, source, :].astype(BF16)
            value = v32[pair, source, :]
            for side in range(2):
                head = 2 * pair + side
                full = jnp.where(left, value, 1.0) if side == 0 else jnp.where(left, 1.0, value)
                va[head, target] = full.astype(BF16)
                if residue == head % seg_count:
                    full = full * 2.0
                vb[head, target] = full.astype(BF16)

    def lanes(side):
        return slice(side * HEAD_WIDTH, (side + 1) * HEAD_WIDTH)

    outer_blocks = (rows - mid) // block
    together = 2 if outer_blocks % 2 == 0 else 1

    def outer(index, carry):
        pair = index // (outer_blocks // together)
        first = index % (outer_blocks // together) * together
        jobs, targets = [], []
        for ahead in range(together):
            for side in range(2):
                head = 2 * pair + side
                own = head % seg_count
                start = ((own + 1) * mid + (first + ahead) * block) % rows
                target = pl.ds(pl.multiple_of(start, block), block)
                jobs.append((qm[head, target], [kp[pair]], [va[head]]))
                targets.append((target, side))
        for (target, side), (total, _) in zip(targets, attend(jobs)):
            outp[pair, target, lanes(side)] = divide(total)[:, lanes(side)]
        return carry

    outer_steps = outer_blocks // together
    lax.fori_loop(0, outer_steps, outer, 0)

    for copy in line_copies:
        copy.wait()
    plane_copies = []
    for step, peer in enumerate(plane_peers):
        copy = pltpu.make_async_remote_copy(
            src_ref=far.at[seg, plane],
            dst_ref=far.at[seg, plane],
            send_sem=plane_send.at[step],
            recv_sem=plane_recv.at[PLANE - 2 - step],
            device_id=(peer, seg),
            device_id_type=MESH,
        )
        copy.start()
        plane_copies.append(copy)
    lax.fori_loop(outer_steps, pairs * outer_steps, outer, 0)

    for copy in mid_copies:
        copy.wait()
    away = (seg_count - 1) * mid
    away_left = left_of(away)
    for pair in range(pairs):
        value = mid_in[:, 1, pair].reshape(away, PAIR).astype(F32)
        vmid[2 * pair] = jnp.where(away_left, value, 1.0).astype(BF16)
        vmid[2 * pair + 1] = jnp.where(away_left, 1.0, value).astype(BF16)

    inner_blocks = mid // block

    def inner(pair, carry):
        away_keys = mid_in[:, 0, pair].reshape(away, PAIR)
        jobs, targets = [], []
        for part in range(inner_blocks):
            for side in range(2):
                head = 2 * pair + side
                start = head % seg_count * mid + part * block
                target = pl.ds(pl.multiple_of(start, block), block)
                jobs.append((qm[head, target], [kp[pair], away_keys], [vb[head], vmid[head]]))
                targets.append((head, target, side, pl.ds(part * block, block)))
        for (head, target, side, kept), (total, highest) in zip(targets, attend(jobs)):
            outp[pair, target, lanes(side)] = divide(total)[:, lanes(side)]
            acc_s[head, kept] = total
            max_s[head, kept] = jnp.broadcast_to(highest, (block, PAIR))
        return carry

    early = pairs - 1
    lax.fori_loop(0, early, inner, 0)

    for copy in plane_copies:
        copy.wait()
    fwd_copies = []
    for step in range(1, seg_count):
        peer = lax.rem(seg + step, seg_count)
        copy = pltpu.make_async_remote_copy(
            src_ref=far.at[seg],
            dst_ref=far.at[seg],
            send_sem=fwd_send.at[step - 1],
            recv_sem=fwd_recv.at[seg_count - 1 - step],
            device_id=(grp, peer),
            device_id_type=MESH,
        )
        copy.start()
        fwd_copies.append(copy)
    lax.fori_loop(early, pairs, inner, 0)
    for copy in fwd_copies:
        copy.wait()

    far_keys_count = seg_count * SLIDE_GRP * far_pad
    wide_left = left_of(far_keys_count)
    jobs = []
    for pair in range(pairs):
        far_keys = far[:, :, :, 0, pair].reshape(far_keys_count, PAIR)
        far_values = far[:, :, :, 1, pair].reshape(far_keys_count, PAIR).astype(F32)
        for side in range(2):
            head = 2 * pair + side
            query = q32[pair, pl.ds(head % period, far_rows, stride=period), :]
            query = jnp.where(far_left == (side == 0), query, 0.0)
            if far_pad > far_rows:
                query = jnp.concatenate([query] * (far_pad // far_rows), axis=0)
            value = jnp.where(wide_left == (side == 0), far_values, 1.0)
            if far_pad > far_rows:
                within = lax.broadcasted_iota(jnp.int32, (far_keys_count, PAIR), 0) % far_pad
                value = jnp.where(within < far_rows, value, 0.0)
            jobs.append((query.astype(BF16), [far_keys], [value.astype(BF16)]))

    results = attend(jobs)
    for pair in range(pairs):
        for side in range(2):
            head = 2 * pair + side
            total, highest = results[head]
            total, highest = total[:far_rows], highest[:far_rows]
            ours = pl.ds(head // seg_count % SLIDE_GRP, far_rows, stride=SLIDE_GRP)
            near_total, near_highest = acc_s[head, ours, :], max_s[head, ours, :]
            ceiling = jnp.maximum(near_highest, highest)
            joined = near_total * jnp.exp(near_highest - ceiling) + total * jnp.exp(
                highest - ceiling
            )
            place_rows = pl.ds(
                head % seg_count * mid + head // seg_count % SLIDE_GRP, far_rows, stride=SLIDE_GRP
            )
            outp[pair, place_rows, :] = jnp.where(
                far_left == (side == 0), divide(joined), outp[pair, place_rows, :]
            )

    o_ref[...] = outp[...].astype(BF16)


def unsort(seg_count, sorted_ref, o_ref, stage):
    pairs, rows, _ = sorted_ref.shape
    mid = rows // seg_count
    for pair in range(pairs):
        for residue in range(seg_count):
            stage[pair, pl.ds(residue, mid, stride=seg_count), :] = sorted_ref[
                pair, pl.ds(residue * mid, mid)
            ].astype(F32)
        o_ref[:, pair * PAIR : (pair + 1) * PAIR] = stage[pair].astype(BF16)


def body(queries, keys, values):
    rows, features = queries.shape
    seg_count = lax.axis_size("seg")
    pairs = features // PAIR
    heads = features // HEAD_WIDTH
    mid = rows // seg_count
    far_rows = rows // (SLIDE_GRP * seg_count)
    far_pad = max(16, far_rows)
    away = (seg_count - 1) * mid
    vmem = pl.BlockSpec(memory_space=pltpu.VMEM)
    dma = pltpu.SemaphoreType.DMA
    ordered = pl.pallas_call(
        functools.partial(kernel, seg_count),
        out_shape=jax.ShapeDtypeStruct((pairs, rows, PAIR), BF16),
        in_specs=[vmem] * 3,
        out_specs=vmem,
        scratch_shapes=[
            pltpu.VMEM((pairs, rows, PAIR), F32),
            pltpu.VMEM((pairs, rows, PAIR), F32),
            pltpu.VMEM((pairs, rows, PAIR), F32),
            pltpu.VMEM((heads, rows, PAIR), BF16),
            pltpu.VMEM((pairs, rows, PAIR), BF16),
            pltpu.VMEM((heads, rows, PAIR), BF16),
            pltpu.VMEM((heads, rows, PAIR), BF16),
            pltpu.VMEM((2, pairs, mid, PAIR), BF16),
            pltpu.VMEM((seg_count - 1, 2, pairs, mid, PAIR), BF16),
            pltpu.VMEM((heads, away, PAIR), BF16),
            pltpu.VMEM((seg_count, PLANE, LINE, 2, pairs, far_pad, PAIR), BF16),
            pltpu.VMEM((pairs, rows, PAIR), F32),
            pltpu.VMEM((heads, mid, PAIR), F32),
            pltpu.VMEM((heads, mid, PAIR), F32),
            dma((seg_count - 1,)),
            dma((seg_count - 1,)),
            dma((LINE - 1,)),
            dma((LINE - 1,)),
            dma((PLANE - 1,)),
            dma((PLANE - 1,)),
            dma((seg_count - 1,)),
            dma((seg_count - 1,)),
        ],
        compiler_params=pltpu.CompilerParams(
            collective_id=0, has_side_effects=True, vmem_limit_bytes=56 * 1024 * 1024
        ),
        name="dilated_attention",
    )(queries, keys, values)
    return pl.pallas_call(
        functools.partial(unsort, seg_count),
        out_shape=jax.ShapeDtypeStruct(queries.shape, BF16),
        in_specs=[vmem],
        out_specs=vmem,
        scratch_shapes=[pltpu.VMEM((pairs, rows, PAIR), F32)],
        compiler_params=pltpu.CompilerParams(vmem_limit_bytes=32 * 1024 * 1024),
        name="token_order",
    )(ordered)


def solution(mesh):
    spec = P(("grp", "seg"), None)
    return jax.shard_map(
        body, mesh=mesh, in_specs=(spec, spec, spec), out_specs=spec, check_vma=False
    )
```

```python
import functools

import jax
import jax.numpy as jnp
from jax import lax
from jax.experimental import pallas as pl
from jax.experimental.pallas import tpu as pltpu
from jax.sharding import PartitionSpec as P

HEAD_WIDTH = 64
PAIR = 2 * HEAD_WIDTH
SLIDE_GRP = 16
LINE = 4
PLANE = SLIDE_GRP // LINE
BLOCK = 256

MESH = pl.DeviceIdType.MESH
F32 = jnp.float32
BF16 = jnp.bfloat16


def scores_of(query, key):
    return lax.dot_general(query, key, (((1,), (1,)), ((), ())), preferred_element_type=F32)


def attend(jobs):
    def scores(job):
        query, keys, _ = job
        return [scores_of(query, key) for key in keys]

    results = []
    ahead = scores(jobs[0])
    for index, (_, _, values) in enumerate(jobs):
        now = ahead
        if index + 1 < len(jobs):
            ahead = scores(jobs[index + 1])
        highest = functools.reduce(
            jnp.maximum, [jnp.max(one, axis=-1, keepdims=True) for one in now]
        )
        total = None
        for one, value in zip(now, values):
            raised = jnp.exp(one - highest).astype(BF16)
            part = jnp.dot(raised, value, preferred_element_type=F32)
            total = part if total is None else total + part
        results.append((total, highest))
    return results


def divide(total):
    return total / pltpu.roll(total, HEAD_WIDTH, 1)


def kernel(
    seg_count,
    q_ref, k_ref, v_ref, o_ref,
    q32, k32, v32, qm, kp, va, vb, mid_out, mid_in, vmid, far, outp, acc_s, max_s,
    mid_send, mid_recv, line_send, line_recv, plane_send, plane_recv, fwd_send, fwd_recv,
):
    rows = q_ref.shape[0]
    pairs = q_ref.shape[1] // PAIR
    mid = rows // seg_count
    period = SLIDE_GRP * seg_count
    far_rows = rows // period
    far_pad = far.shape[5]
    block = min(BLOCK, mid)
    grp, seg = lax.axis_index("grp"), lax.axis_index("seg")
    place = lax.rem(grp, SLIDE_GRP)
    base = grp - place
    line, plane = place // PLANE, lax.rem(place, PLANE)

    barrier = pltpu.get_barrier_semaphore()
    line_peers = [
        base + lax.rem(line + step, LINE) * PLANE + plane for step in range(1, LINE)
    ]
    plane_peers = [
        base + line * PLANE + lax.rem(plane + step, PLANE) for step in range(1, PLANE)
    ]
    for peer in line_peers + plane_peers:
        pl.semaphore_signal(barrier, inc=1, device_id=(peer, seg), device_id_type=MESH)
    for step in range(1, seg_count):
        peer = lax.rem(seg + step, seg_count)
        pl.semaphore_signal(barrier, inc=1, device_id=(grp, peer), device_id_type=MESH)

    def left_of(count):
        return lax.broadcasted_iota(jnp.int32, (count, PAIR), 1) < HEAD_WIDTH

    left = left_of(mid)
    far_left = left_of(far_rows)

    def far_slot(array, pair):
        picked = jnp.where(
            far_left,
            array[pair, pl.ds((2 * pair) % period, far_rows, stride=period), :],
            array[pair, pl.ds((2 * pair + 1) % period, far_rows, stride=period), :],
        )
        if far_pad > far_rows:
            picked = jnp.concatenate([picked] * (far_pad // far_rows), axis=0)
        return picked.astype(BF16)

    for pair in range(pairs):
        columns = slice(pair * PAIR, (pair + 1) * PAIR)
        even, odd = (2 * pair) % seg_count, (2 * pair + 1) % seg_count
        k32[pair] = k_ref[:, columns].astype(F32)
        v32[pair] = v_ref[:, columns].astype(F32)
        mid_out[0, pair] = jnp.where(
            left,
            k32[pair, pl.ds(even, mid, stride=seg_count), :],
            k32[pair, pl.ds(odd, mid, stride=seg_count), :],
        ).astype(BF16)
        mid_out[1, pair] = jnp.where(
            left,
            v32[pair, pl.ds(even, mid, stride=seg_count), :],
            v32[pair, pl.ds(odd, mid, stride=seg_count), :],
        ).astype(BF16)
        far[seg, plane, line, 0, pair] = far_slot(k32, pair)
        far[seg, plane, line, 1, pair] = far_slot(v32, pair)

    pl.semaphore_wait(barrier, LINE - 1 + PLANE - 1 + seg_count - 1)

    mid_copies = []
    for step in range(1, seg_count):
        peer = lax.rem(seg + step, seg_count)
        copy = pltpu.make_async_remote_copy(
            src_ref=mid_out,
            dst_ref=mid_in.at[seg_count - 1 - step],
            send_sem=mid_send.at[step - 1],
            recv_sem=mid_recv.at[seg_count - 1 - step],
            device_id=(grp, peer),
            device_id_type=MESH,
        )
        copy.start()
        mid_copies.append(copy)
    line_copies = []
    for step, peer in enumerate(line_peers):
        copy = pltpu.make_async_remote_copy(
            src_ref=far.at[seg, plane, line],
            dst_ref=far.at[seg, plane, line],
            send_sem=line_send.at[step],
            recv_sem=line_recv.at[LINE - 2 - step],
            device_id=(peer, seg),
            device_id_type=MESH,
        )
        copy.start()
        line_copies.append(copy)

    for pair in range(pairs):
        columns = slice(pair * PAIR, (pair + 1) * PAIR)
        q32[pair] = q_ref[:, columns].astype(F32) * HEAD_WIDTH ** (-0.5)
        for residue in range(seg_count):
            target = pl.ds(residue * mid, mid)
            source = pl.ds(residue, mid, stride=seg_count)
            query = q32[pair, source, :]
            qm[2 * pair, target] = jnp.where(left, query, 0.0).astype(BF16)
            qm[2 * pair + 1, target] = jnp.where(left, 0.0, query).astype(BF16)
            kp[pair, target] = k32[pair, source, :].astype(BF16)
            value = v32[pair, source, :]
            for side in range(2):
                head = 2 * pair + side
                full = jnp.where(left, value, 1.0) if side == 0 else jnp.where(left, 1.0, value)
                va[head, target] = full.astype(BF16)
                if residue == head % seg_count:
                    full = full * 2.0
                vb[head, target] = full.astype(BF16)

    def lanes(side):
        return slice(side * HEAD_WIDTH, (side + 1) * HEAD_WIDTH)

    outer_blocks = (rows - mid) // block
    together = 2 if outer_blocks % 2 == 0 else 1

    def outer(index, carry):
        pair = index // (outer_blocks // together)
        first = index % (outer_blocks // together) * together
        jobs, targets = [], []
        for ahead in range(together):
            for side in range(2):
                head = 2 * pair + side
                own = head % seg_count
                start = ((own + 1) * mid + (first + ahead) * block) % rows
                target = pl.ds(pl.multiple_of(start, block), block)
                jobs.append((qm[head, target], [kp[pair]], [va[head]]))
                targets.append((target, side))
        for (target, side), (total, _) in zip(targets, attend(jobs)):
            outp[pair, target, lanes(side)] = divide(total)[:, lanes(side)]
        return carry

    outer_steps = outer_blocks // together
    lax.fori_loop(0, outer_steps, outer, 0)

    for copy in line_copies:
        copy.wait()
    plane_copies = []
    for step, peer in enumerate(plane_peers):
        copy = pltpu.make_async_remote_copy(
            src_ref=far.at[seg, plane],
            dst_ref=far.at[seg, plane],
            send_sem=plane_send.at[step],
            recv_sem=plane_recv.at[PLANE - 2 - step],
            device_id=(peer, seg),
            device_id_type=MESH,
        )
        copy.start()
        plane_copies.append(copy)
    lax.fori_loop(outer_steps, pairs * outer_steps, outer, 0)

    for copy in mid_copies:
        copy.wait()
    away = (seg_count - 1) * mid
    away_left = left_of(away)
    for pair in range(pairs):
        value = mid_in[:, 1, pair].reshape(away, PAIR)
        ones = jnp.ones_like(value)
        vmid[2 * pair] = jnp.where(away_left, value, ones)
        vmid[2 * pair + 1] = jnp.where(away_left, ones, value)

    inner_blocks = mid // block

    def inner(pair, carry):
        away_keys = mid_in[:, 0, pair].reshape(away, PAIR)
        jobs, targets = [], []
        for part in range(inner_blocks):
            for side in range(2):
                head = 2 * pair + side
                start = head % seg_count * mid + part * block
                target = pl.ds(pl.multiple_of(start, block), block)
                jobs.append((qm[head, target], [kp[pair], away_keys], [vb[head], vmid[head]]))
                targets.append((head, target, side, pl.ds(part * block, block)))
        for (head, target, side, kept), (total, highest) in zip(targets, attend(jobs)):
            outp[pair, target, lanes(side)] = divide(total)[:, lanes(side)]
            acc_s[head, kept] = total
            max_s[head, kept] = jnp.broadcast_to(highest, (block, PAIR))
        return carry

    early = pairs - 1
    lax.fori_loop(0, early, inner, 0)

    for copy in plane_copies:
        copy.wait()
    fwd_copies = []
    for step in range(1, seg_count):
        peer = lax.rem(seg + step, seg_count)
        copy = pltpu.make_async_remote_copy(
            src_ref=far.at[seg],
            dst_ref=far.at[seg],
            send_sem=fwd_send.at[step - 1],
            recv_sem=fwd_recv.at[seg_count - 1 - step],
            device_id=(grp, peer),
            device_id_type=MESH,
        )
        copy.start()
        fwd_copies.append(copy)
    lax.fori_loop(early, pairs, inner, 0)
    for copy in fwd_copies:
        copy.wait()

    far_keys_count = seg_count * SLIDE_GRP * far_pad
    wide_left = left_of(far_keys_count)
    jobs = []
    for pair in range(pairs):
        far_keys = far[:, :, :, 0, pair].reshape(far_keys_count, PAIR)
        far_values = far[:, :, :, 1, pair].reshape(far_keys_count, PAIR)
        for side in range(2):
            head = 2 * pair + side
            query = q32[pair, pl.ds(head % period, far_rows, stride=period), :]
            query = jnp.where(far_left == (side == 0), query, 0.0)
            if far_pad > far_rows:
                query = jnp.concatenate([query] * (far_pad // far_rows), axis=0)
            ones = jnp.ones_like(far_values)
            value = jnp.where(wide_left, *((far_values, ones) if side == 0 else (ones, far_values)))
            if far_pad > far_rows:
                within = lax.broadcasted_iota(jnp.int32, (far_keys_count, PAIR), 0) % far_pad
                value = jnp.where(within < far_rows, value, jnp.zeros_like(value))
            jobs.append((query.astype(BF16), [far_keys], [value]))

    results = attend(jobs)
    for pair in range(pairs):
        for side in range(2):
            head = 2 * pair + side
            total, highest = results[head]
            total, highest = total[:far_rows], highest[:far_rows]
            ours = pl.ds(head // seg_count % SLIDE_GRP, far_rows, stride=SLIDE_GRP)
            near_total, near_highest = acc_s[head, ours, :], max_s[head, ours, :]
            ceiling = jnp.maximum(near_highest, highest)
            joined = near_total * jnp.exp(near_highest - ceiling) + total * jnp.exp(
                highest - ceiling
            )
            place_rows = pl.ds(
                head % seg_count * mid + head // seg_count % SLIDE_GRP, far_rows, stride=SLIDE_GRP
            )
            outp[pair, place_rows, :] = jnp.where(
                far_left == (side == 0), divide(joined), outp[pair, place_rows, :]
            )

    o_ref[...] = outp[...].astype(BF16)


def unsort(seg_count, sorted_ref, o_ref, stage):
    pairs, rows, _ = sorted_ref.shape
    mid = rows // seg_count
    for pair in range(pairs):
        for residue in range(seg_count):
            stage[pair, pl.ds(residue, mid, stride=seg_count), :] = sorted_ref[
                pair, pl.ds(residue * mid, mid)
            ].astype(F32)
        o_ref[:, pair * PAIR : (pair + 1) * PAIR] = stage[pair].astype(BF16)


def body(queries, keys, values):
    rows, features = queries.shape
    seg_count = lax.axis_size("seg")
    pairs = features // PAIR
    heads = features // HEAD_WIDTH
    mid = rows // seg_count
    far_rows = rows // (SLIDE_GRP * seg_count)
    far_pad = max(16, far_rows)
    away = (seg_count - 1) * mid
    vmem = pl.BlockSpec(memory_space=pltpu.VMEM)
    dma = pltpu.SemaphoreType.DMA
    ordered = pl.pallas_call(
        functools.partial(kernel, seg_count),
        out_shape=jax.ShapeDtypeStruct((pairs, rows, PAIR), BF16),
        in_specs=[vmem] * 3,
        out_specs=vmem,
        scratch_shapes=[
            pltpu.VMEM((pairs, rows, PAIR), F32),
            pltpu.VMEM((pairs, rows, PAIR), F32),
            pltpu.VMEM((pairs, rows, PAIR), F32),
            pltpu.VMEM((heads, rows, PAIR), BF16),
            pltpu.VMEM((pairs, rows, PAIR), BF16),
            pltpu.VMEM((heads, rows, PAIR), BF16),
            pltpu.VMEM((heads, rows, PAIR), BF16),
            pltpu.VMEM((2, pairs, mid, PAIR), BF16),
            pltpu.VMEM((seg_count - 1, 2, pairs, mid, PAIR), BF16),
            pltpu.VMEM((heads, away, PAIR), BF16),
            pltpu.VMEM((seg_count, PLANE, LINE, 2, pairs, far_pad, PAIR), BF16),
            pltpu.VMEM((pairs, rows, PAIR), F32),
            pltpu.VMEM((heads, mid, PAIR), F32),
            pltpu.VMEM((heads, mid, PAIR), F32),
            dma((seg_count - 1,)),
            dma((seg_count - 1,)),
            dma((LINE - 1,)),
            dma((LINE - 1,)),
            dma((PLANE - 1,)),
            dma((PLANE - 1,)),
            dma((seg_count - 1,)),
            dma((seg_count - 1,)),
        ],
        compiler_params=pltpu.CompilerParams(
            collective_id=0, has_side_effects=True, vmem_limit_bytes=56 * 1024 * 1024
        ),
        name="dilated_attention",
    )(queries, keys, values)
    return pl.pallas_call(
        functools.partial(unsort, seg_count),
        out_shape=jax.ShapeDtypeStruct(queries.shape, BF16),
        in_specs=[vmem],
        out_specs=vmem,
        scratch_shapes=[pltpu.VMEM((pairs, rows, PAIR), F32)],
        compiler_params=pltpu.CompilerParams(vmem_limit_bytes=32 * 1024 * 1024),
        name="token_order",
    )(ordered)


def solution(mesh):
    spec = P(("grp", "seg"), None)
    return jax.shard_map(
        body, mesh=mesh, in_specs=(spec, spec, spec), out_specs=spec, check_vma=False
    )
```
